256 devices in a mesh: step: 4 (over z_hi, core), seq: 64 (over z_lo, y, x).
Axes of the slice: x: 4, y: 4, z: 8 (z_hi: 2, z_lo: 4; z = z_hi * 4 + z_lo), core: 2. Of those that a mesh axis runs over, the one named last changes fastest.
Arguments:
- joined: bfloat16 [8192, 7168], P('seq'), may hold values from -6 to 6
- drafted: bfloat16 [4, 8192, 7168], P('step', 'seq'), may hold values from -6 to 6
- queries: bfloat16 [4, 8192, 3584], P('step', 'seq')
- norm_gain: bfloat16 [7168], replicated, may hold values from 0.099609375 to 1.8984375
- key_matrix: bfloat16 [7168, 512], P('seq', 'step'), may hold values from -0.0625 to 0.0625
- value_matrix: bfloat16 [7168, 512], P('seq', 'step'), may hold values from -0.0625 to 0.0625
Outputs:
- attended: bfloat16 [4, 8192, 3584], P('step', 'seq')
The draws below stay inside these ranges and needn't reach their ends.
All inputs are finite; a program needn't handle non-finite values.
Results may differ from the reference program's by a relative error of at most 0.006.
The reference program's roundings to bfloat16 on the way count: a program that leaves them out, or rounds other values in their place, can miss the bound.
Values may be sent and summed in bfloat16 or wider, within the bound.
A program may use at most 128 MiB of HBM per device.

```python
import math
import jax
import jax.numpy as jnp
from jax import lax

D = 7168
QH = 28
KVH = 4
HD = 128
L = 8192
STEPS = 4


def draw_queries(key, part):
    key = jax.random.fold_in(key, 7)
    shape = (STEPS, L, QH * HD)
    values = jax.random.normal(jax.random.fold_in(key, 1), shape, jnp.float32)
    return values.astype(jnp.bfloat16)


def levels(stream_key, dims, split, low, top_value):
    level = 1.0
    for axis_at, shards_of in split:
        steps = jax.random.uniform(jax.random.fold_in(jax.random.fold_in(stream_key, 6), axis_at), (shards_of,), jnp.float32, low / len(split), top_value / len(split))
        level = level * jnp.repeat(jnp.exp(steps), dims[axis_at] // shards_of).reshape((-1,) + (1,) * (len(dims) - 1 - axis_at))
    return level


def bell_draw(own_key, shape, scale, most, cuts=(), held_as=jnp.bfloat16):
    array = jax.random.normal(own_key, shape, jnp.float32) * scale
    if len(cuts) > 0:
        array = levels(own_key, shape, cuts, -0.22, 0.18) * array
    return jnp.clip(array, min=-most, max=most).astype(held_as)


def setup_inputs(seed: int = 0) -> dict:
    splits = jax.random.split(jax.random.key(seed), 7)
    return {
        "joined": bell_draw(splits[0], (L, D), 1.0, 6.0, ((0, 64),)),
        "drafted": bell_draw(splits[1], (STEPS, L, D), 1.0, 6.0, ((0, 4), (1, 64))),
        "queries": draw_queries(jax.random.fold_in(splits[6], 71), 0),
        "norm_gain": jnp.clip(1.0 + 0.18 * jax.random.normal(splits[3], (D,), jnp.float32), 0.099609375, 1.8984375).astype(jnp.bfloat16),
        "key_matrix": bell_draw(splits[4], (D, KVH * HD), D ** -0.5, 0.0625, ((0, 64), (1, 4))),
        "value_matrix": bell_draw(splits[5], (D, KVH * HD), D ** -0.5, 0.0625, ((0, 64), (1, 4))),
    }


def normed(rows, gain):
    values = rows.astype(jnp.float32)
    scaled = values * lax.rsqrt(lax.optimization_barrier(jnp.mean(values * values, axis=-1, keepdims=True)) + 1e-06)
    return (scaled * gain.astype(jnp.float32)).astype(jnp.bfloat16)

def reference(joined, drafted, queries, norm_gain, key_matrix, value_matrix):
    group = QH // KVH
    scale = HD ** (-0.5)
    context_normed = normed(joined, norm_gain)
    context_keys = jnp.dot(context_normed, key_matrix, preferred_element_type=jnp.float32).astype(jnp.bfloat16)
    context_values = jnp.dot(context_normed, value_matrix, preferred_element_type=jnp.float32).astype(jnp.bfloat16)
    context_keys = context_keys.astype(jnp.float32).reshape(L, KVH, HD)
    context_values = context_values.astype(jnp.float32).reshape(L, KVH, HD)
    drafted_hidden_normalized = normed(drafted, norm_gain).astype(jnp.float32)
    per_step_keys = jnp.einsum('pyf,fh->pyh', drafted_hidden_normalized, key_matrix.astype(jnp.float32)).astype(jnp.bfloat16)
    per_step_values = jnp.einsum('pyf,fh->pyh', drafted_hidden_normalized, value_matrix.astype(jnp.float32)).astype(jnp.bfloat16)
    per_step_keys = per_step_keys.astype(jnp.float32).reshape(STEPS, L, KVH, HD)
    per_step_values = per_step_values.astype(jnp.float32).reshape(STEPS, L, KVH, HD)
    block = math.gcd(L, 512)
    key_pos = jnp.arange(L, dtype=jnp.int32)
    outputs = []
    for step in range(STEPS):

        def one_block(index):
            first = (index * block).astype(jnp.int32)
            query_rows = lax.dynamic_slice_in_dim(queries[step], first, block, 0)
            query_rows = query_rows.astype(jnp.float32).reshape(block, KVH, group, HD)
            scores = jnp.einsum('tkgd,nkd->tkgn', query_rows, context_keys) * scale
            query_offset = first + jnp.arange(block, dtype=jnp.int32)
            allowed = key_pos[None, :] <= query_offset[:, None]
            scores = jnp.where(allowed[:, None, None, :], scores, -1e+30)
            own_keys = lax.dynamic_slice_in_dim(per_step_keys, first, block, 1)
            drafter_values = lax.dynamic_slice_in_dim(per_step_values, first, block, 1)
            diag = jnp.einsum('tkgd,jtkd->tkgj', query_rows, own_keys) * scale
            live = jnp.arange(STEPS) <= step
            diag = jnp.where(live[None, None, None, :], diag, -1e+30)
            top = jnp.maximum(lax.optimization_barrier(jnp.max(scores, axis=-1)), lax.optimization_barrier(jnp.max(diag, axis=-1)))
            weights = jnp.exp(scores - top[..., None])
            diag_weights = jnp.exp(diag - top[..., None])
            total = lax.optimization_barrier(jnp.sum(weights, axis=-1)) + lax.optimization_barrier(jnp.sum(diag_weights, axis=-1))
            rounded = weights.astype(jnp.bfloat16).astype(jnp.float32)
            diag_rounded = diag_weights.astype(jnp.bfloat16).astype(jnp.float32)
            summed = jnp.einsum('tkgn,nkd->tkgd', rounded, context_values)
            summed = summed + jnp.einsum('tkgj,jtkd->tkgd', diag_rounded, drafter_values)
            result = summed / total[..., None]
            return result.reshape(block, QH * HD).astype(jnp.bfloat16)
        blocks = lax.map(one_block, jnp.arange(L // block, dtype=jnp.int32))
        outputs.append(blocks.reshape(L, QH * HD))
    return jnp.stack(outputs)
```

```python
import functools
import math

import jax
import jax.numpy as jnp
from jax import lax
from jax.experimental import pallas as pl
from jax.experimental.pallas import tpu as pltpu
from jax.sharding import PartitionSpec as P

QH = 28
KVH = 4
HD = 128
GROUP = QH // KVH
D = 7168
TOK = 128
STEPS = 4
ROWS = 112
SIZE = {"x": 4, "y": 4, "z": 8}
ORDER = {"A": "zyx", "B": "zxy", "C": "xyz"}
W_ROWS = {"A": 80, "B": 64, "C": 80}
KV_ROWS = {"A": 48, "B": 48, "C": 32}
MESH = pl.DeviceIdType.MESH
LOG2E = math.log2(math.e)
NEG = -1e30


def position():
    step = lax.axis_index("step")
    seq = lax.axis_index("seq")
    return {
        "z": (step // 2) * 4 + seq // 16,
        "y": lax.rem(seq // 4, 4),
        "x": lax.rem(seq, 4),
        "core": lax.rem(step, 2),
    }


def device(at, **moved):
    at = dict(at)
    for axis, by in moved.items():
        size = SIZE.get(axis, 2)
        at[axis] = lax.rem(at[axis] + by + size, size)
    return (
        (at["z"] // 4) * 2 + at["core"],
        lax.rem(at["z"], 4) * 16 + at["y"] * 4 + at["x"],
    )


def hops(size, split):
    found = []
    for hop in range(1, size // 2):
        found += [(1, hop, None), (-1, hop, None)]
    last = size // 2
    return found + ([(1, last, 0), (-1, last, 1)] if split else [(1, last, None)])


def gather_plan(shard_bytes):
    plan = {}
    for piece, (a1, a2, a3) in ORDER.items():
        n1, n2, n3 = SIZE[a1], SIZE[a2], SIZE[a3]
        unit = shard_bytes[piece]
        first = [(piece, 1, 0, d, k) for d, k, _ in hops(n1, False)]
        for d, k, _ in hops(n1, False):
            plan[piece, 1, 0, d, k] = ((a1, d), unit, [(piece, 1, 0, d, k - 1)] if k > 1 else [])
        for d, k, half in hops(n2, True):
            need = [(piece, 2, 0, d, k - 1)] if k > 1 else first
            plan[piece, 2, 0, d, k] = ((a2, d), unit * n1 // (1 if half is None else 2), need)
        for sub in (0, 1, -1, 2):
            begin = {
                0: first,
                1: [(piece, 2, 0, -1, 1)],
                -1: [(piece, 2, 0, 1, 1)],
                2: [(piece, 2, 0, 1, 2), (piece, 2, 0, -1, 2)],
            }[sub]
            for d, k, half in hops(n3, True):
                need = [(piece, 3, sub, d, k - 1)] if k > 1 else begin
                plan[piece, 3, sub, d, k] = (
                    (a3, d),
                    unit * n1 // (1 if half is None else 2),
                    need,
                )
        for off in range(n3):
            if off == 0:
                need = first + [(piece, 2, 0, d, k) for d, k, _ in hops(n2, True)]
            else:
                need = [
                    (piece, 3, sub, d, k)
                    for sub in (0, 1, -1, 2)
                    for d, k, _ in hops(n3, True)
                    if (-d * k) % n3 == off
                ]
            plan[piece, "core", off] = (("core", 0), unit * n1 * n2, need)
    return plan


def simulate(plan):
    arrive = {}
    free = {}
    waiting = dict(plan)
    while waiting:
        ready = []
        for name, (link, size, need) in waiting.items():
            if all(other in arrive for other in need):
                ready.append((max([arrive[other] for other in need], default=0.0), name))
        ready.sort(key=lambda pair: pair[0])
        at, name = ready[0]
        link, size, _ = waiting.pop(name)
        begin = max(at, free.get(link, 0.0))
        rate = 400e3 if link[0] == "core" else 43e3
        free[link] = begin + size / rate
        arrive[name] = free[link] + 1.0
    return sorted(plan, key=lambda name: arrive[name]), arrive


class Gather:
    def __init__(self, bufs, at, send, recv, base, shard_bytes):
        self.bufs, self.at = bufs, at
        self.send, self.recv, self.base = send, recv, base
        self.plan = gather_plan(shard_bytes)
        self.index = {name: base + i for i, name in enumerate(self.plan)}
        self.order, self.arrive = simulate(self.plan)
        self.got = set()
        self.sent = set()

    def copy(self, name, incoming):
        at = self.at
        buf = self.bufs[name[0]]
        a1, a2, a3 = ORDER[name[0]]
        c = at["core"]
        if name[1] == "core":
            n3 = SIZE[a3]
            q3 = lax.rem(at[a3] + name[2], n3)
            ref = buf.at[1 - c if incoming else c, q3]
            target = device(at, core=1)
        else:
            piece, phase, sub, d, k = name
            axis = ORDER[piece][phase - 1]
            n = SIZE[axis]
            n1 = SIZE[a1]
            back = k if incoming else k - 1
            q = lax.rem(at[axis] - d * back + n, n)
            half = None
            if phase > 1 and k == n // 2:
                half = 0 if d > 0 else 1
            inner = pl.ds(0, n1) if half is None else pl.ds(half * (n1 // 2), n1 // 2)
            if phase == 1:
                ref = buf.at[c, at[a3], at[a2], q]
            elif phase == 2:
                ref = buf.at[c, at[a3], q, inner]
            else:
                q2 = lax.rem(at[a2] + sub + SIZE[a2], SIZE[a2])
                ref = buf.at[c, q, q2, inner]
            target = device(at, **{axis: d})
        i = self.index[name]
        return pltpu.make_async_remote_copy(
            src_ref=ref,
            dst_ref=ref,
            send_sem=self.send.at[i],
            recv_sem=self.recv.at[i],
            device_id=target,
            device_id_type=MESH,
        )

    def start_ready(self):
        for name, (_, _, need) in self.plan.items():
            if name not in self.sent and all(other in self.got for other in need):
                self.sent.add(name)
                self.copy(name, False).start()

    def run(self, tasks=()):
        tasks = list(tasks)
        now = 0.0
        self.start_ready()
        for name in self.order:
            while tasks and now + tasks[0][0] <= self.arrive[name] + 0.3:
                cost, task = tasks.pop(0)
                now += cost
                task()
            now = max(now, self.arrive[name])
            self.copy(name, True).wait_recv()
            self.got.add(name)
            self.start_ready()
        for _, task in tasks:
            task()

    def finish(self):
        for name in self.plan:
            self.copy(name, False).wait_send()


def kernel(
    joined_ref, drafted_ref, queries_ref, gain_ref, key_ref, value_ref, out_ref,
    wa, wb, wc, ka, kb, kc, diag, rows_in, normed, q_held, acc, top, proj, ctx,
    local_sem, w_send, w_recv, k_send, k_recv, d_send, d_recv,
):
    at = position()
    x, y, z, c = at["x"], at["y"], at["z"], at["core"]
    step = lax.axis_index("step")
    z_hi = z // 4
    z_lo = lax.rem(z, 4)

    load_rows = [
        pltpu.make_async_copy(joined_ref, rows_in.at[0], local_sem.at[0]),
        pltpu.make_async_copy(drafted_ref.at[0], rows_in.at[1], local_sem.at[1]),
    ]
    load_q = pltpu.make_async_copy(queries_ref.at[0], q_held, local_sem.at[2])
    for load in load_rows:
        load.start()
    load_q.start()

    wa[c, x, y, z] = key_ref[0:80]
    wb[c, y, x, z, 0:32] = key_ref[80:ROWS]
    wb[c, y, x, z, 32:64] = value_ref[0:32]
    wc[c, z, y, x] = value_ref[32:ROWS]

    barrier = pltpu.get_barrier_semaphore()
    partners = [device(at, x=1), device(at, x=-1), device(at, y=1), device(at, y=-1)]
    partners += [device(at, z=1), device(at, z=-1), device(at, core=1), device(at, z=4)]
    for partner in partners:
        pl.semaphore_signal(barrier, inc=1, device_id=partner, device_id_type=MESH)
    pl.semaphore_wait(barrier, len(partners))

    def norm_rows(which, first, count):
        def body(i, carry):
            start = pl.multiple_of(first + i * 16, 16)
            rows = rows_in[which, pl.ds(start, 16), :].astype(jnp.float32)
            mean = jnp.sum(rows * rows, axis=-1, keepdims=True) * (1.0 / D)
            scaled = rows * lax.rsqrt(mean + 1e-06)
            normed[which, pl.ds(start, 16), :] = (
                scaled * gain_ref[...].astype(jnp.float32)
            ).astype(jnp.bfloat16)
            return carry

        lax.fori_loop(0, count // 16, body, 0)

    def norm_task(which, first):
        def task():
            if first == 0:
                load_rows[which].wait()
            norm_rows(which, first, 32)

        return task

    weights = Gather(
        {"A": wa, "B": wb, "C": wc}, at, w_send, w_recv, 0,
        {piece: rows * HD * 2 for piece, rows in W_ROWS.items()},
    )
    weights.run([(1.0, norm_task(which, 32 * i)) for which in range(2) for i in range(4)])

    proj[...] = jnp.zeros_like(proj)
    ctx[...] = jnp.zeros_like(ctx)

    def project(zz, carry):
        cols = pl.ds(pl.multiple_of(lax.rem(zz, 4) * (16 * ROWS), 128), 16 * ROWS)
        drafted_part = normed[1, :, cols]
        for cc in range(2):
            head = (zz // 4) * 2 + cc
            keys, values = [], []
            for yy in range(4):
                for xx in range(4):
                    keys += [wa[cc, xx, yy, zz], wb[cc, yy, xx, zz, 0:32]]
                    values += [wb[cc, yy, xx, zz, 32:64], wc[cc, zz, yy, xx]]
            both = jnp.concatenate(
                [jnp.concatenate(keys, axis=0), jnp.concatenate(values, axis=0)], axis=1
            )
            proj[head] += jnp.dot(drafted_part, both, preferred_element_type=jnp.float32)

            @pl.when(head == step)
            def _():
                ctx[...] += jnp.dot(
                    normed[0, :, cols], both, preferred_element_type=jnp.float32
                )

        return carry

    lax.fori_loop(0, 8, project, 0)

    held = ctx[...].astype(jnp.bfloat16)
    for kv in range(2):
        part = held[:, kv * HD : (kv + 1) * HD]
        ka[c, x, y, z, kv] = part[0:48]
        kb[c, y, x, z, kv] = part[48:96]
        kc[c, z, y, x, kv] = part[96:128]

    def store_diag(head, carry):
        both = proj[head].astype(jnp.bfloat16)
        for kv in range(2):
            diag[step, head, kv] = both[:, kv * HD : (kv + 1) * HD]
        return carry

    lax.fori_loop(0, KVH, store_diag, 0)

    def diag_copy(which, sem, target):
        return pltpu.make_async_remote_copy(
            src_ref=diag.at[which],
            dst_ref=diag.at[which],
            send_sem=d_send.at[sem],
            recv_sem=d_recv.at[sem],
            device_id=target,
            device_id_type=MESH,
        )

    sibling = device(at, core=1)
    sibling_step = z_hi * 2 + 1 - c
    other = device(at, z=4)
    diag_copy(step, 0, sibling).start()

    @pl.when(z_hi == 0)
    def _():
        diag_copy(step, 1, other).start()

    context = Gather(
        {"A": ka, "B": kb, "C": kc}, at, k_send, k_recv, 0,
        {piece: 2 * rows * HD * 2 for piece, rows in KV_ROWS.items()},
    )
    context.run()
    diag_copy(sibling_step, 0, sibling).wait_recv()

    @pl.when(z_hi == 1)
    def _():
        diag_copy(c, 1, other).wait_recv()
        diag_copy(c, 2, sibling).start()
        diag_copy(1 - c, 2, sibling).wait_recv()
        diag_copy(c, 2, sibling).wait_send()

    diag_copy(step, 0, sibling).wait_send()

    @pl.when(z_hi == 0)
    def _():
        diag_copy(step, 1, other).wait_send()

    load_q.wait()

    acc[...] = jnp.zeros_like(acc)
    top[...] = jnp.full_like(top, NEG)
    scale = LOG2E * HD ** (-0.5)
    row = lax.broadcasted_iota(jnp.int32, (TOK, 1), 0)
    my_seq = lax.axis_index("seq")

    def attend(head, keys, values, bias):
        count = keys.shape[0]
        wide = jnp.concatenate([values, jnp.ones((count, HD), jnp.bfloat16)], axis=1)
        for g in range(GROUP):
            q = q_held[:, pl.ds(pl.multiple_of((head * GROUP + g) * HD, HD), HD)]
            scores = lax.dot_general(
                q, keys, (((1,), (1,)), ((), ())), preferred_element_type=jnp.float32
            ) * scale
            if bias is not None:
                scores = scores + bias
            old = top[head, g]
            new = jnp.maximum(old, jnp.max(scores, axis=-1, keepdims=True))
            top[head, g] = new
            fade = jnp.exp2(old - new)
            p = jnp.exp2(scores - jnp.concatenate([new] * (count // HD), axis=1))
            acc[head, g] = acc[head, g] * jnp.concatenate([fade, fade], axis=1) + jnp.dot(
                p.astype(jnp.bfloat16), wide, preferred_element_type=jnp.float32
            )

    def diag_head(head, carry):
        for pair in range(2):
            keys = diag[pl.ds(2 * pair, 2), head, 0].reshape(2 * TOK, HD)
            values = diag[pl.ds(2 * pair, 2), head, 1].reshape(2 * TOK, HD)
            col = lax.broadcasted_iota(jnp.int32, (TOK, 2 * TOK), 1)
            j = 2 * pair + col // TOK
            ok = jnp.logical_and(lax.rem(col, TOK) == row, j <= step)
            bias = jnp.where(ok, 0.0, NEG)
            ok_rows = j <= step
            attend(head, keys, values, bias)
        return carry

    def key_seq(piece, zz, count, rows):
        col = lax.broadcasted_iota(jnp.int32, (1, count), 1)
        shard = col // rows
        within = lax.rem(col, rows)
        outer, inner = shard // 4, lax.rem(shard, 4)
        if piece == "A":
            xx, yy = outer, inner
        else:
            yy, xx = outer, inner
        start = {"A": 0, "B": 48, "C": 96}[piece]
        return (zz * 16 + yy * 4 + xx) * TOK + start + within

    def plane(zz, masked):
        def body(head, carry):
            zed = (head // 2) * 4 + zz
            core = lax.rem(head, 2)
            for piece, buf in (("A", ka), ("B", kb), ("C", kc)):
                rows = KV_ROWS[piece]
                count = 16 * rows
                if piece == "C":
                    keys = buf[core, zed, :, :, 0].reshape(count, HD)
                    values = buf[core, zed, :, :, 1].reshape(count, HD)
                else:
                    keys = buf[core, :, :, zed, 0].reshape(count, HD)
                    values = buf[core, :, :, zed, 1].reshape(count, HD)
                bias = None
                if masked:
                    ok = key_seq(piece, zz, count, rows) <= my_seq * TOK + row
                    bias = jnp.where(ok, 0.0, NEG)
                attend(head, keys, values, bias)
            return carry

        lax.fori_loop(0, KVH, body, 0)

    lax.fori_loop(0, KVH, diag_head, 0)
    lax.fori_loop(0, z_lo, lambda zz, carry: (plane(zz, False), carry)[1], 0)
    plane(z_lo, True)

    def write(head, carry):
        for g in range(GROUP):
            both = acc[head, g]
            q_held[:, pl.ds(pl.multiple_of((head * GROUP + g) * HD, HD), HD)] = (
                both[:, :HD] / both[:, HD:]
            ).astype(jnp.bfloat16)
        return carry

    lax.fori_loop(0, KVH, write, 0)
    store = pltpu.make_async_copy(q_held, out_ref.at[0], local_sem.at[3])
    store.start()
    weights.finish()
    context.finish()
    store.wait()


def per_device(joined, drafted, queries, norm_gain, key_matrix, value_matrix):
    messages = len(gather_plan({"A": 1, "B": 1, "C": 1}))
    bf16 = jnp.bfloat16
    any_space = pl.BlockSpec(memory_space=pl.ANY)
    vmem = pl.BlockSpec(memory_space=pltpu.VMEM)
    dma = pltpu.SemaphoreType.DMA
    return pl.pallas_call(
        kernel,
        out_shape=jax.ShapeDtypeStruct((1, TOK, QH * HD), bf16),
        in_specs=[any_space, any_space, any_space, vmem, vmem, vmem],
        out_specs=any_space,
        scratch_shapes=[
            pltpu.VMEM((2, 4, 4, 8, 80, HD), bf16),
            pltpu.VMEM((2, 4, 4, 8, 64, HD), bf16),
            pltpu.VMEM((2, 8, 4, 4, 80, HD), bf16),
            pltpu.VMEM((2, 4, 4, 8, 2, 48, HD), bf16),
            pltpu.VMEM((2, 4, 4, 8, 2, 48, HD), bf16),
            pltpu.VMEM((2, 8, 4, 4, 2, 32, HD), bf16),
            pltpu.VMEM((STEPS, KVH, 2, TOK, HD), bf16),
            pltpu.VMEM((2, TOK, D), bf16),
            pltpu.VMEM((2, TOK, D), bf16),
            pltpu.VMEM((TOK, QH * HD), bf16),
            pltpu.VMEM((KVH, GROUP, TOK, 2 * HD), jnp.float32),
            pltpu.VMEM((KVH, GROUP, TOK, HD), jnp.float32),
            pltpu.VMEM((KVH, TOK, 2 * HD), jnp.float32),
            pltpu.VMEM((TOK, 2 * HD), jnp.float32),
            dma((4,)),
            dma((messages,)),
            dma((messages,)),
            dma((messages,)),
            dma((messages,)),
            dma((3,)),
            dma((3,)),
        ],
        compiler_params=pltpu.CompilerParams(
            collective_id=0, has_side_effects=True, vmem_limit_bytes=60 * 2**20
        ),
        cost_estimate=pl.CostEstimate(
            flops=17 * 10**9, bytes_accessed=8 * 10**6, transcendentals=3 * 10**7
        ),
        name="drafter",
    )(joined, drafted, queries, norm_gain.reshape(1, D), key_matrix, value_matrix)


def solution(mesh):
    placed = (
        P("seq", None),
        P("step", "seq", None),
        P("step", "seq", None),
        P(),
        P("seq", "step"),
        P("seq", "step"),
    )
    return jax.shard_map(
        per_device, mesh=mesh, in_specs=placed, out_specs=P("step", "seq", None), check_vma=False
    )
```

```python
import math

import jax
import jax.numpy as jnp
from jax import lax
from jax.experimental import pallas as pl
from jax.experimental.pallas import tpu as pltpu
from jax.sharding import PartitionSpec as P

QH = 28
KVH = 4
HD = 128
GROUP = QH // KVH
D = 7168
TOK = 128
STEPS = 4
ROWS = 112
SIZE = {"x": 4, "y": 4, "z": 8}
ORDER = {"A": "zyx", "B": "zxy", "C": "xyz"}
W_ROWS = {"A": 80, "B": 64, "C": 80}
KV_ROWS = {"A": 48, "B": 48, "C": 32}
MESH = pl.DeviceIdType.MESH
LOG2E = math.log2(math.e)
NEG = -1e30


def position():
    step = lax.axis_index("step")
    seq = lax.axis_index("seq")
    return {
        "z": (step // 2) * 4 + seq // 16,
        "y": lax.rem(seq // 4, 4),
        "x": lax.rem(seq, 4),
        "core": lax.rem(step, 2),
    }


def device(at, **moved):
    at = dict(at)
    for axis, by in moved.items():
        size = SIZE.get(axis, 2)
        at[axis] = lax.rem(at[axis] + by + size, size)
    return (
        (at["z"] // 4) * 2 + at["core"],
        lax.rem(at["z"], 4) * 16 + at["y"] * 4 + at["x"],
    )


def hops(size):
    found = []
    for hop in range(1, size // 2):
        found += [(1, hop, None), (-1, hop, None)]
    last = size // 2
    return found + [(1, last, 0), (-1, last, 1)]


def near_first(size):
    return sorted(range(1, size), key=lambda k: min(k, size - k))


def gather_plan(tag, shard_bytes, begin):
    plan = {}
    for piece, (a1, a2, a3) in ORDER.items():
        n1, n2, n3 = SIZE[a1], SIZE[a2], SIZE[a3]
        unit = shard_bytes[piece]
        key = (tag, piece)
        first = [key + (1, 0, 1, k) for k in range(1, n1)]
        for k in near_first(n1):
            plan[key + (1, 0, 1, k)] = (
                (a1, 1 if k <= n1 // 2 else -1),
                unit * min(k, n1 - k),
                begin,
            )
        for d, k, half in hops(n2):
            need = [key + (2, 0, d, k - 1)] if k > 1 else first
            plan[key + (2, 0, d, k)] = ((a2, d), unit * n1 // (1 if half is None else 2), need)
        for sub in (0, 1, -1, 2):
            start = {
                0: first,
                1: [key + (2, 0, -1, 1)],
                -1: [key + (2, 0, 1, 1)],
                2: [key + (2, 0, 1, 2), key + (2, 0, -1, 2)],
            }[sub]
            for d, k, half in hops(n3):
                need = [key + (3, sub, d, k - 1)] if k > 1 else start
                plan[key + (3, sub, d, k)] = (
                    (a3, d),
                    unit * n1 // (1 if half is None else 2),
                    need,
                )
    return plan


def plane_needs(tag, piece, off):
    a1, a2, a3 = ORDER[piece]
    key = (tag, piece)
    if off == 0:
        return [key + (1, 0, 1, k) for k in range(1, SIZE[a1])] + [
            key + (2, 0, d, k) for d, k, _ in hops(SIZE[a2])
        ]
    return [
        key + (3, sub, d, k)
        for sub in (0, 1, -1, 2)
        for d, k, _ in hops(SIZE[a3])
        if (-d * k) % SIZE[a3] == off
    ]


LATENCY, RATE, CORE_RATE, HANDLE = 3.0, 43e3, 400e3, 0.15


def schedule(plan, tasks):
    steps = []
    done = set()
    link_free = {}
    arrive = {}
    unsent = dict(plan)
    todo = dict(tasks)
    now = 0.0

    def send_ready():
        for name in sorted(unsent, key=lambda name: (name[2], name[5])):
            link, size, need = plan[name]
            if all(other in done for other in need):
                del unsent[name]
                steps.append(("send", name))
                rate = CORE_RATE if link[0] == "core" else RATE
                begin = max(now, link_free.get(link, 0.0))
                link_free[link] = begin + size / rate
                arrive[name] = link_free[link] + LATENCY

    send_ready()
    while arrive or todo:
        early = min(arrive, key=lambda name: arrive[name], default=None)
        ready = next((t for t, (_, need) in todo.items() if all(o in done for o in need)), None)
        if early is not None and (arrive[early] <= now or ready is None):
            now = max(now, arrive.pop(early)) + HANDLE
            steps.append(("wait", early))
            done.add(early)
        else:
            now += todo.pop(ready)[0]
            steps.append(("task", ready))
            done.add(ready)
        send_ready()
    return steps, now


def kernel(
    joined_ref, drafted_ref, queries_ref, gain_ref, key_ref, value_ref, out_ref,
    wa, wb, wc, ka, kb, kc, diag, rows_in, normed, q_held, o_held, acc, top, proj, ctx,
    local_sem, send_sem, recv_sem,
):
    at = position()
    x, y, z, c = at["x"], at["y"], at["z"], at["core"]
    step = lax.axis_index("step")
    seq = lax.axis_index("seq")
    z_hi = z // 4
    z_lo = lax.rem(z, 4)
    sibling = device(at, core=1)
    antipode = device(at, z=4)

    def columns(head):
        return pl.ds(pl.multiple_of(head * (GROUP * HD), HD), GROUP * HD)

    load_rows = [
        pltpu.make_async_copy(drafted_ref.at[0], rows_in.at[0], local_sem.at[0]),
        pltpu.make_async_copy(joined_ref, rows_in.at[1], local_sem.at[1]),
    ]
    load_q = [
        pltpu.make_async_copy(
            queries_ref.at[0, :, columns(c + 2 * hh)], q_held.at[c, hh], local_sem.at[2 + hh]
        )
        for hh in range(2)
    ]
    for load in load_rows + load_q:
        load.start()

    wa[x, y, z] = key_ref[0:80]
    wb[y, x, z, 0:32] = key_ref[80:ROWS]
    wb[y, x, z, 32:64] = value_ref[0:32]
    wc[z, y, x] = value_ref[32:ROWS]

    barrier = pltpu.get_barrier_semaphore()
    partners = [device(at, x=k) for k in range(1, 4)] + [device(at, z=k) for k in range(1, 8)]
    partners += [device(at, y=1), device(at, y=-1), sibling]
    for partner in partners:
        pl.semaphore_signal(barrier, inc=1, device_id=partner, device_id_type=MESH)
    pl.semaphore_wait(barrier, len(partners))

    plan = {}
    for i in range(2):
        plan["core", "q", 0, 0, 0, i] = (("core", 0), TOK * GROUP * HD * 2, [])
        plan["core", "rows", 0, 0, 0, i] = (("core", 0), TOK * D, [("norm", 0, i)])
    plan.update(
        gather_plan("w", {piece: rows * HD * 2 for piece, rows in W_ROWS.items()}, [])
    )
    plan.update(
        gather_plan(
            "kv", {piece: 2 * rows * HD * 2 for piece, rows in KV_ROWS.items()}, [("project", 0)]
        )
    )
    index = {name: i for i, name in enumerate(plan)}
    bufs = {
        ("w", "A"): wa, ("w", "B"): wb, ("w", "C"): wc,
        ("kv", "A"): ka, ("kv", "B"): kb, ("kv", "C"): kc,
    }

    def remote(src, dst, i, target):
        return pltpu.make_async_remote_copy(
            src_ref=src,
            dst_ref=dst,
            send_sem=send_sem.at[i],
            recv_sem=recv_sem.at[i],
            device_id=target,
            device_id_type=MESH,
        )

    def copy(name, incoming):
        tag, piece, phase, sub, d, k = name
        i = index[name]
        if tag == "core":
            mine = 1 - c if incoming else c
            if piece == "rows":
                ref = normed.at[mine, pl.ds(k * 64, 64)]
                return remote(ref, ref, i, sibling)
            src = queries_ref.at[0, :, columns(1 - c + 2 * k)]
            return remote(src, q_held.at[mine, k], i, sibling)
        buf = bufs[tag, piece]
        a1, a2, a3 = ORDER[piece]
        axis = ORDER[piece][phase - 1]
        n, n1 = SIZE[axis], SIZE[a1]
        q = lax.rem(at[axis] - d * (k if incoming else k - 1) + n, n)
        half = None
        if phase > 1 and k == n // 2:
            half = 0 if d > 0 else 1
        inner = pl.ds(0, n1) if half is None else pl.ds(half * (n1 // 2), n1 // 2)
        if phase == 1:
            mine = lax.rem(at[axis] - k + n, n) if incoming else at[axis]
            ref = buf.at[at[a3], at[a2], mine]
            return remote(ref, ref, i, device(at, **{axis: k}))
        if phase == 2:
            ref = buf.at[at[a3], q, inner]
        else:
            ref = buf.at[q, lax.rem(at[a2] + sub + SIZE[a2], SIZE[a2]), inner]
        return remote(ref, ref, i, device(at, **{axis: d}))

    count = len(plan)
    far = remote(diag.at[pl.ds(0, 2)], diag.at[pl.ds(0, 2)], count, antipode)

    def norm(which, first):
        if first == 0:
            load_rows[which].wait()

        def body(i, carry):
            start = pl.multiple_of(first + i * 16, 16)
            rows = rows_in[which, pl.ds(start, 16), :].astype(jnp.float32)
            mean = jnp.sum(rows * rows, axis=-1, keepdims=True) * (1.0 / D)
            scaled = rows * lax.rsqrt(mean + 1e-06)
            done = (scaled * gain_ref[...].astype(jnp.float32)).astype(jnp.bfloat16)
            normed[c if which == 0 else 2, pl.ds(start, 16), :] = done
            return carry

        lax.fori_loop(0, 4, body, 0)

    def project():
        proj[...] = jnp.zeros_like(proj)
        ctx[...] = jnp.zeros_like(ctx)

        def part(zz, carry):
            hh = zz // 4
            cols = pl.ds(pl.multiple_of(lax.rem(zz, 4) * (16 * ROWS), 128), 16 * ROWS)
            keys, values = [], []
            for yy in range(4):
                for xx in range(4):
                    keys += [wa[xx, yy, zz], wb[yy, xx, zz, 0:32]]
                    values += [wb[yy, xx, zz, 32:64], wc[zz, yy, xx]]
            both = jnp.concatenate(
                [jnp.concatenate(keys, axis=0), jnp.concatenate(values, axis=0)], axis=1
            )
            drafted_part = normed[0:2, :, cols].reshape(2 * TOK, 16 * ROWS)
            proj[hh] += jnp.dot(drafted_part, both, preferred_element_type=jnp.float32)

            @pl.when(hh == z_hi)
            def _():
                ctx[...] += jnp.dot(normed[2, :, cols], both, preferred_element_type=jnp.float32)

            return carry

        lax.fori_loop(0, 8, part, 0)
        held = ctx[...].astype(jnp.bfloat16)
        for kv in range(2):
            part = held[:, kv * HD : (kv + 1) * HD]
            ka[x, y, z, kv] = part[0:48]
            kb[y, x, z, kv] = part[48:96]
            kc[z, y, x, kv] = part[96:128]
        for st in range(2):
            for hh in range(2):
                both = proj[hh, pl.ds(st * TOK, TOK)].astype(jnp.bfloat16)
                for kv in range(2):
                    diag[2 * z_hi + st, hh, kv] = both[:, kv * HD : (kv + 1) * HD]

    def send_far():
        @pl.when(z_hi == 0)
        def _():
            far.start()

    scale = LOG2E * HD ** (-0.5)
    row = lax.broadcasted_iota(jnp.int32, (TOK, 1), 0)

    def attend(hh, keys, values, bias):
        count = keys.shape[0]
        wide = jnp.concatenate([values, jnp.ones((count, HD), jnp.bfloat16)], axis=1)
        for st in range(2):
            mine = bias(st) if callable(bias) else bias
            for g in range(GROUP):
                q = q_held[st, hh, :, g * HD : (g + 1) * HD]
                scores = lax.dot_general(
                    q, keys, (((1,), (1,)), ((), ())), preferred_element_type=jnp.float32
                ) * scale
                if mine is not None:
                    scores = scores + mine
                old = top[hh, st, g]
                new = jnp.maximum(old, jnp.max(scores, axis=-1, keepdims=True))
                top[hh, st, g] = new
                fade = jnp.exp2(old - new)
                p = jnp.exp2(scores - jnp.concatenate([new] * (count // HD), axis=1))
                acc[hh, st, g] = acc[hh, st, g] * jnp.concatenate([fade, fade], axis=1) + jnp.dot(
                    p.astype(jnp.bfloat16), wide, preferred_element_type=jnp.float32
                )

    def attend_diag(pair, hh):
        keys, values = (
            diag[pl.ds(2 * pair, 2), hh, kv].reshape(2 * TOK, HD) for kv in range(2)
        )
        col = lax.broadcasted_iota(jnp.int32, (TOK, 2 * TOK), 1)
        j = 2 * pair + col // TOK

        def bias(st):
            ok = jnp.logical_and(lax.rem(col, TOK) == row, j <= 2 * z_hi + st)
            return jnp.where(ok, 0.0, NEG)

        attend(hh, keys, values, bias)

    def attend_plane(piece, off, hh):
        rows = KV_ROWS[piece]
        count = 16 * rows
        col = lax.broadcasted_iota(jnp.int32, (1, count), 1)
        shard = col // rows
        outer, inner = shard // 4, lax.rem(shard, 4)
        if piece == "C":
            zed = lax.rem(z + off, 8)
            hh = zed // 4
            keys, values = (kc[zed, :, :, kv].reshape(count, HD) for kv in range(2))
            where = (lax.rem(zed, 4), outer, inner)
        else:
            plane = lax.rem(at[ORDER[piece][2]] + off, 4)
            buf = ka if piece == "A" else kb
            keys, values = (
                buf[plane, :, 4 * hh : 4 * hh + 4, kv].reshape(count, HD) for kv in range(2)
            )
            where = (inner, outer, plane) if piece == "A" else (inner, plane, outer)
        zz, yy, xx = where
        start = {"A": 0, "B": 48, "C": 96}[piece]
        key_at = (zz * 16 + yy * 4 + xx) * TOK + start + lax.rem(col, rows)
        bias = jnp.where(key_at <= seq * TOK + row, 0.0, NEG)
        if piece == "C":

            @pl.when(zz <= z_lo)
            def _():
                attend(hh, keys, values, bias)

        else:
            attend(hh, keys, values, bias)

    tasks = {}
    for which in range(2):
        for i in range(2):
            tasks["norm", which, i] = (2.2, [])
    tasks["project", 0] = (
        5.0,
        list(tasks)
        + [name for name in plan if name[0] == "w"]
        + [name for name in plan if name[:2] == ("core", "rows")],
    )
    tasks["far", 0] = (0.1, [("project", 0)])
    for hh in range(2):
        tasks["diag far", hh] = (1.4, [("far", 0), ("kv", "A", 3, 0, 1, 1)])
    for hh in range(2):
        tasks["diag", hh] = (1.4, [("project", 0)])
    for off in (0, 1, -1, 2, -2, 3, -3, 4):
        for piece in "ABC":
            if piece == "C" or -2 < off < 3:
                need = plane_needs("kv", piece, off % SIZE[ORDER[piece][2]])
                for hh in range(1 if piece == "C" else 2):
                    tasks["attend", piece, off % SIZE[ORDER[piece][2]], hh] = (
                        KV_ROWS[piece] / 48 * 2.1,
                        need,
                    )

    steps, _ = schedule(plan, tasks)
    acc[...] = jnp.zeros_like(acc)
    top[...] = jnp.full_like(top, NEG)
    for kind, name in steps:
        if kind == "send":
            copy(name, False).start()
        elif kind == "wait":
            copy(name, True).wait_recv()
        elif name[0] == "norm":
            norm(name[1], 64 * name[2])
        elif name[0] == "project":
            project()
        elif name[0] == "far":
            send_far()
        elif name[0] == "diag":
            if name[1] == 0:
                for load in load_q:
                    load.wait()
            attend_diag(z_hi, name[1])
        elif name[0] == "diag far":

            @pl.when(z_hi == 1)
            def _():
                if name[1] == 0:
                    far.wait_recv()
                attend_diag(0, name[1])

        else:
            attend_plane(*name[1:])

    def out_copy(hh, own):
        src = o_held.at[c if own else 1 - c, hh]
        dst = out_ref.at[0, :, columns(c + 2 * hh)]
        if own:
            return pltpu.make_async_copy(src, dst, local_sem.at[4 + hh])
        return remote(src, dst, count + 1 + hh, sibling)

    def out_wait(hh):
        dst = out_ref.at[0, :, columns(1 - c + 2 * hh)]
        return remote(o_held.at[c, hh], dst, count + 1 + hh, sibling)

    for hh in range(2):
        def write(st, carry):
            for g in range(GROUP):
                both = acc[hh, st, g]
                o_held[st, hh, :, g * HD : (g + 1) * HD] = (
                    both[:, :HD] / both[:, HD:]
                ).astype(jnp.bfloat16)
            return carry

        lax.fori_loop(0, 2, write, 0)
        out_copy(hh, False).start()
        out_copy(hh, True).start()
    for name in plan:
        copy(name, False).wait_send()

    @pl.when(z_hi == 0)
    def _():
        far.wait_send()

    for hh in range(2):
        out_copy(hh, True).wait()
        out_copy(hh, False).wait_send()
        out_wait(hh).wait_recv()


def per_device(joined, drafted, queries, norm_gain, key_matrix, value_matrix):
    unit = {"A": 1, "B": 1, "C": 1}
    messages = 2 * len(gather_plan("w", unit, [])) + 4 + 3
    bf16 = jnp.bfloat16
    any_space = pl.BlockSpec(memory_space=pl.ANY)
    vmem = pl.BlockSpec(memory_space=pltpu.VMEM)
    dma = pltpu.SemaphoreType.DMA
    return pl.pallas_call(
        kernel,
        out_shape=jax.ShapeDtypeStruct((1, TOK, QH * HD), bf16),
        in_specs=[any_space, any_space, any_space, vmem, vmem, vmem],
        out_specs=any_space,
        scratch_shapes=[
            pltpu.VMEM((4, 4, 8, 80, HD), bf16),
            pltpu.VMEM((4, 4, 8, 64, HD), bf16),
            pltpu.VMEM((8, 4, 4, 80, HD), bf16),
            pltpu.VMEM((4, 4, 8, 2, 48, HD), bf16),
            pltpu.VMEM((4, 4, 8, 2, 48, HD), bf16),
            pltpu.VMEM((8, 4, 4, 2, 32, HD), bf16),
            pltpu.VMEM((STEPS, 2, 2, TOK, HD), bf16),
            pltpu.VMEM((2, TOK, D), bf16),
            pltpu.VMEM((3, TOK, D), bf16),
            pltpu.VMEM((2, 2, TOK, GROUP * HD), bf16),
            pltpu.VMEM((2, 2, TOK, GROUP * HD), bf16),
            pltpu.VMEM((2, 2, GROUP, TOK, 2 * HD), jnp.float32),
            pltpu.VMEM((2, 2, GROUP, TOK, HD), jnp.float32),
            pltpu.VMEM((2, 2 * TOK, 2 * HD), jnp.float32),
            pltpu.VMEM((TOK, 2 * HD), jnp.float32),
            dma((6,)),
            dma((messages,)),
            dma((messages,)),
        ],
        compiler_params=pltpu.CompilerParams(
            collective_id=0, has_side_effects=True, vmem_limit_bytes=60 * 2**20
        ),
        cost_estimate=pl.CostEstimate(
            flops=17 * 10**9, bytes_accessed=8 * 10**6, transcendentals=3 * 10**7
        ),
        name="drafter",
    )(joined, drafted, queries, norm_gain.reshape(1, D), key_matrix, value_matrix)


def solution(mesh):
    placed = (
        P("seq", None),
        P("step", "seq", None),
        P("step", "seq", None),
        P(),
        P("seq", "step"),
        P("seq", "step"),
    )
    return jax.shard_map(
        per_device, mesh=mesh, in_specs=placed, out_specs=P("step", "seq", None), check_vma=False
    )
```

```python
import math

import jax
import jax.numpy as jnp
from jax import lax
from jax.experimental import pallas as pl
from jax.experimental.pallas import tpu as pltpu
from jax.sharding import PartitionSpec as P

QH = 28
KVH = 4
HD = 128
GROUP = QH // KVH
D = 7168
TOK = 128
STEPS = 4
ROWS = 112
SIZE = {"x": 4, "y": 4, "z": 8}
ORDER = {"A": "zyx", "B": "zxy", "C": "xyz"}
W_ROWS = {"A": 80, "B": 64, "C": 80}
KV_ROWS = {"A": 48, "B": 32, "C": 48}
KV_START = {"A": 0, "B": 48, "C": 80}
MESH = pl.DeviceIdType.MESH
LOG2E = math.log2(math.e)
NEG = -1e30


def position():
    step = lax.axis_index("step")
    seq = lax.axis_index("seq")
    return {
        "z": (step // 2) * 4 + seq // 16,
        "y": lax.rem(seq // 4, 4),
        "x": lax.rem(seq, 4),
        "core": lax.rem(step, 2),
    }


def device(at, **moved):
    at = dict(at)
    for axis, by in moved.items():
        size = SIZE.get(axis, 2)
        at[axis] = lax.rem(at[axis] + by + size, size)
    return (
        (at["z"] // 4) * 2 + at["core"],
        lax.rem(at["z"], 4) * 16 + at["y"] * 4 + at["x"],
    )


def hops(size):
    found = []
    for hop in range(1, size // 2):
        found += [(1, hop, None), (-1, hop, None)]
    last = size // 2
    return found + [(1, last, 0), (-1, last, 1)]


def near_first(size):
    return sorted(range(1, size), key=lambda k: min(k, size - k))


def gather_plan(tag, shard_bytes, begin):
    plan = {}
    for piece, (a1, a2, a3) in ORDER.items():
        n1, n2, n3 = SIZE[a1], SIZE[a2], SIZE[a3]
        unit = shard_bytes[piece]
        key = (tag, piece)
        first = [key + (1, 0, 1, k) for k in range(1, n1)]
        for k in near_first(n1):
            plan[key + (1, 0, 1, k)] = (
                (a1, 1 if k <= n1 // 2 else -1),
                unit * min(k, n1 - k),
                begin,
            )
        for d, k, half in hops(n2):
            need = [key + (2, 0, d, k - 1)] if k > 1 else first
            plan[key + (2, 0, d, k)] = ((a2, d), unit * n1 // (1 if half is None else 2), need)
        for sub in (0, 1, -1, 2):
            start = {
                0: first,
                1: [key + (2, 0, -1, 1)],
                -1: [key + (2, 0, 1, 1)],
                2: [key + (2, 0, 1, 2), key + (2, 0, -1, 2)],
            }[sub]
            if piece != "C" and sub == 0:
                start = start + [(tag, other, 1, 0, 1, k) for other in "AB" for k in range(1, n1)]
            elif piece != "C":
                other = "B" if piece == "A" else "A"
                start = start + [(tag, other, 2, 0, d, 1) for d in (1, -1)]
            for d, k, half in hops(n3):
                need = [key + (3, sub, d, k - 1)] if k > 1 else start
                plan[key + (3, sub, d, k)] = (
                    (a3, d),
                    unit * n1 // (1 if half is None else 2),
                    need,
                )
    return plan


def plane_needs(tag, piece, off):
    a1, a2, a3 = ORDER[piece]
    key = (tag, piece)
    if off == 0:
        return [key + (1, 0, 1, k) for k in range(1, SIZE[a1])] + [
            key + (2, 0, d, k) for d, k, _ in hops(SIZE[a2])
        ]
    return [
        key + (3, sub, d, k)
        for sub in (0, 1, -1, 2)
        for d, k, _ in hops(SIZE[a3])
        if (-d * k) % SIZE[a3] == off
    ]


LATENCY, RATE, CORE_RATE, HANDLE = 3.0, 42e3, 400e3, 0.05


def schedule(plan, tasks):
    steps = []
    done = set()
    link_free = {}
    arrive = {}
    unsent = dict(plan)
    todo = dict(tasks)
    now = 0.0

    def send_ready():
        for name in sorted(unsent, key=lambda name: (name[2], name[5])):
            link, size, need = plan[name]
            if all(other in done for other in need):
                del unsent[name]
                steps.append(("send", name))
                rate = CORE_RATE if link[0] == "core" else RATE
                begin = max(now, link_free.get(link, 0.0))
                link_free[link] = begin + size / rate
                arrive[name] = link_free[link] + LATENCY

    send_ready()
    while arrive or todo:
        early = min(arrive, key=lambda name: arrive[name], default=None)
        ready = next((t for t, (_, need) in todo.items() if all(o in done for o in need)), None)
        if early is not None and (arrive[early] <= now or ready is None):
            now = max(now, arrive.pop(early)) + HANDLE
            steps.append(("wait", early))
            done.add(early)
        else:
            now += todo.pop(ready)[0]
            steps.append(("task", ready))
            done.add(ready)
        send_ready()
    return steps, now


def kernel(
    joined_ref, drafted_ref, queries_ref, gain_ref, key_ref, value_ref, out_ref,
    wa, wb, wc, ka, kb, kc, diag, rows_in, normed, q_held, o_held, acc, top, proj, ctx,
    gain_held, local_sem, send_sem, recv_sem,
):
    at = position()
    x, y, z, c = at["x"], at["y"], at["z"], at["core"]
    step = lax.axis_index("step")
    seq = lax.axis_index("seq")
    z_hi = z // 4
    z_lo = lax.rem(z, 4)
    sibling = device(at, core=1)
    antipode = device(at, z=4)

    def columns(head):
        return pl.ds(pl.multiple_of(head * (GROUP * HD), HD), GROUP * HD)

    load_rows = [
        pltpu.make_async_copy(drafted_ref.at[0], rows_in.at[0], local_sem.at[0]),
        pltpu.make_async_copy(joined_ref, rows_in.at[1], local_sem.at[1]),
    ]
    load_q = [
        pltpu.make_async_copy(
            queries_ref.at[0, :, columns(c + 2 * hh)], q_held.at[c, hh], local_sem.at[2 + hh]
        )
        for hh in range(2)
    ]
    for load in load_rows + load_q:
        load.start()

    wa[x, y, z] = key_ref[0:80]
    wb[y, x, z, 0:32] = key_ref[80:ROWS]
    wb[y, x, z, 32:64] = value_ref[0:32]
    wc[z, y, x] = value_ref[32:ROWS]

    gain_held[...] = gain_ref[...].astype(jnp.float32).reshape(1, D)
    barrier = pltpu.get_barrier_semaphore()
    partners = [device(at, x=k) for k in range(1, 4)] + [device(at, z=k) for k in range(1, 8)]
    partners += [device(at, y=1), device(at, y=-1), sibling]
    for partner in partners:
        pl.semaphore_signal(barrier, inc=1, device_id=partner, device_id_type=MESH)
    pl.semaphore_wait(barrier, len(partners))

    plan = {}
    for i in range(2):
        plan["core", "q", 0, 0, 0, i] = (("core", 0), TOK * GROUP * HD * 2, [])
        plan["core", "rows", 0, 0, 0, i] = (("core", 0), TOK * D, [("norm", 0, i)])
    plan.update(
        gather_plan("w", {piece: rows * HD * 2 for piece, rows in W_ROWS.items()}, [])
    )
    plan.update(
        gather_plan(
            "kv", {piece: 2 * rows * HD * 2 for piece, rows in KV_ROWS.items()}, [("project", 0)]
        )
    )
    index = {name: i for i, name in enumerate(plan)}
    bufs = {
        ("w", "A"): wa, ("w", "B"): wb, ("w", "C"): wc,
        ("kv", "A"): ka, ("kv", "B"): kb, ("kv", "C"): kc,
    }

    def remote(src, dst, i, target):
        return pltpu.make_async_remote_copy(
            src_ref=src,
            dst_ref=dst,
            send_sem=send_sem.at[i],
            recv_sem=recv_sem.at[i],
            device_id=target,
            device_id_type=MESH,
        )

    def copy(name, incoming):
        tag, piece, phase, sub, d, k = name
        i = index[name]
        if tag == "core":
            mine = 1 - c if incoming else c
            if piece == "rows":
                ref = normed.at[mine, pl.ds(k * 64, 64)]
                return remote(ref, ref, i, sibling)
            src = queries_ref.at[0, :, columns(1 - c + 2 * k)]
            return remote(src, q_held.at[mine, k], i, sibling)
        buf = bufs[tag, piece]
        a1, a2, a3 = ORDER[piece]
        axis = ORDER[piece][phase - 1]
        n, n1 = SIZE[axis], SIZE[a1]
        q = lax.rem(at[axis] - d * (k if incoming else k - 1) + n, n)
        half = None
        if phase > 1 and k == n // 2:
            half = 0 if d > 0 else 1
        inner = pl.ds(0, n1) if half is None else pl.ds(half * (n1 // 2), n1 // 2)
        if phase == 1:
            mine = lax.rem(at[axis] - k + n, n) if incoming else at[axis]
            ref = buf.at[at[a3], at[a2], mine]
            return remote(ref, ref, i, device(at, **{axis: k}))
        if phase == 2:
            ref = buf.at[at[a3], q, inner]
        else:
            ref = buf.at[q, lax.rem(at[a2] + sub + SIZE[a2], SIZE[a2]), inner]
        return remote(ref, ref, i, device(at, **{axis: d}))

    count = len(plan)
    far = remote(diag.at[pl.ds(0, 2)], diag.at[pl.ds(0, 2)], count, antipode)

    def norm(which, first):
        if first == 0:
            load_rows[which].wait()

        def body(i, carry):
            start = pl.multiple_of(first + i * 16, 16)
            rows = rows_in[which, pl.ds(start, 16), :].astype(jnp.float32)
            mean = jnp.sum(rows * rows, axis=-1, keepdims=True) * (1.0 / D)
            scaled = rows * lax.rsqrt(mean + 1e-06)
            done = (scaled * gain_held[...]).astype(jnp.bfloat16)
            normed[c if which == 0 else 2, pl.ds(start, 16), :] = done
            return carry

        lax.fori_loop(0, 4, body, 0)

    def project():
        proj[...] = jnp.zeros_like(proj)
        ctx[...] = jnp.zeros_like(ctx)

        def part(zz, carry):
            hh = zz // 4
            cols = pl.ds(pl.multiple_of(lax.rem(zz, 4) * (16 * ROWS), 128), 16 * ROWS)
            keys, values = [], []
            for yy in range(4):
                for xx in range(4):
                    keys += [wa[xx, yy, zz], wb[yy, xx, zz, 0:32]]
                    values += [wb[yy, xx, zz, 32:64], wc[zz, yy, xx]]
            both = jnp.concatenate(
                [jnp.concatenate(keys, axis=0), jnp.concatenate(values, axis=0)], axis=1
            )
            drafted_part = normed[0:2, :, cols].reshape(2 * TOK, 16 * ROWS)
            proj[hh] += jnp.dot(drafted_part, both, preferred_element_type=jnp.float32)

            @pl.when(hh == z_hi)
            def _():
                ctx[...] += jnp.dot(normed[2, :, cols], both, preferred_element_type=jnp.float32)

            return carry

        lax.fori_loop(0, 8, part, 0)
        held = ctx[...].astype(jnp.bfloat16)
        for kv in range(2):
            part = held[:, kv * HD : (kv + 1) * HD]
            ka[x, y, z, kv] = part[0:48]
            kb[y, x, z, kv] = part[48:80]
            kc[z, y, x, kv] = part[80:128]
        for st in range(2):
            for hh in range(2):
                both = proj[hh, pl.ds(st * TOK, TOK)].astype(jnp.bfloat16)
                for kv in range(2):
                    diag[2 * z_hi + st, hh, kv] = both[:, kv * HD : (kv + 1) * HD]

    def send_far():
        @pl.when(z_hi == 0)
        def _():
            far.start()

    scale = LOG2E * HD ** (-0.5)
    row = lax.broadcasted_iota(jnp.int32, (TOK, 1), 0)

    def attend(hh, keys, values, bias):
        count = keys.shape[0]
        wide = jnp.concatenate([values, jnp.ones((count, HD), jnp.bfloat16)], axis=1)

        def score(pair):
            tiles = [divmod(2 * pair + i, GROUP) for i in range(2)]
            q = jnp.concatenate(
                [q_held[st, hh, :, g * HD : (g + 1) * HD] for st, g in tiles], axis=0
            )
            scores = lax.dot_general(
                q, keys, (((1,), (1,)), ((), ())), preferred_element_type=jnp.float32
            ) * scale + jnp.concatenate([bias[st] for st, _ in tiles], axis=0)
            old = top[hh, pair]
            new = jnp.maximum(old, jnp.max(scores, axis=-1, keepdims=True))
            top[hh, pair] = new
            return scores, old, new

        def weigh(pair, scores, old, new):
            fade = jnp.exp2(old - new)
            p = jnp.exp2(scores - jnp.concatenate([new] * (count // HD), axis=1))
            acc[hh, pair] = acc[hh, pair] * jnp.concatenate([fade, fade], axis=1) + jnp.dot(
                p.astype(jnp.bfloat16), wide, preferred_element_type=jnp.float32
            )

        held = score(0)
        for pair in range(GROUP):
            following = score(pair + 1) if pair + 1 < GROUP else None
            weigh(pair, *held)
            held = following

    def attend_diag(pair, hh):
        keys, values = (
            diag[pl.ds(2 * pair, 2), hh, kv].reshape(2 * TOK, HD) for kv in range(2)
        )
        col = lax.broadcasted_iota(jnp.int32, (TOK, 2 * TOK), 1)
        j = 2 * pair + col // TOK

        own = lax.rem(col, TOK) == row
        bias = [
            jnp.where(jnp.logical_and(own, j <= 2 * z_hi + st), 0.0, NEG) for st in range(2)
        ]
        attend(hh, keys, values, bias)

    def attend_plane(piece, off):
        rows = KV_ROWS[piece]
        count = 16 * rows
        col = lax.broadcasted_iota(jnp.int32, (1, count), 1)
        shard = col // rows
        outer, inner = shard // 4, lax.rem(shard, 4)
        if piece == "C":
            zed = lax.rem(z + off, 8)
            hh = zed // 4
            keys, values = (kc[zed, :, :, kv].reshape(count, HD) for kv in range(2))
            where = (lax.rem(zed, 4), outer, inner)
        else:
            plane = lax.rem(at[ORDER[piece][2]] + off, 4)
            buf = ka if piece == "A" else kb
            where = (inner, outer, plane) if piece == "A" else (inner, plane, outer)
        zz, yy, xx = where
        key_at = (zz * 16 + yy * 4 + xx) * TOK + KV_START[piece] + lax.rem(col, rows)
        bias = [jnp.where(key_at <= seq * TOK + row, 0.0, NEG)] * 2
        if piece == "C":

            @pl.when(zz <= z_lo)
            def _():
                attend(hh, keys, values, bias)

        else:

            def head(hh, carry):
                keys, values = (
                    buf[plane, :, pl.ds(4 * hh, 4), kv].reshape(count, HD) for kv in range(2)
                )
                attend(hh, keys, values, bias)
                return carry

            lax.fori_loop(0, 2, head, 0)

    tasks = {}
    for which in range(2):
        for i in range(2):
            tasks["norm", which, i] = (2.2, [])
    tasks["project", 0] = (
        5.0,
        list(tasks)
        + [name for name in plan if name[0] == "w"]
        + [name for name in plan if name[:2] == ("core", "rows")],
    )
    tasks["far", 0] = (0.1, [("project", 0)])
    for hh in range(2):
        tasks["diag far", hh] = (0.8, [("far", 0), ("kv", "A", 3, 0, 1, 1)])
    for hh in range(2):
        tasks["diag", hh] = (0.8, [("project", 0)])
    for off in (0, 1, -1, 2, -2, 3, -3, 4):
        for piece in "ABC":
            if piece == "C" or -2 < off < 3:
                need = plane_needs("kv", piece, off % SIZE[ORDER[piece][2]])
                cost = KV_ROWS[piece] / 48 * (1.75 if piece == "C" else 3.5)
                tasks["attend", piece, off % SIZE[ORDER[piece][2]]] = (cost, need)

    steps, _ = schedule(plan, tasks)
    acc[...] = jnp.zeros_like(acc)
    top[...] = jnp.full_like(top, NEG)
    for kind, name in steps:
        if kind == "send":
            copy(name, False).start()
        elif kind == "wait":
            copy(name, True).wait_recv()
        elif name[0] == "norm":
            norm(name[1], 64 * name[2])
        elif name[0] == "project":
            project()
        elif name[0] == "far":
            send_far()
        elif name[0] == "diag":
            if name[1] == 0:
                for load in load_q:
                    load.wait()
            attend_diag(z_hi, name[1])
        elif name[0] == "diag far":

            @pl.when(z_hi == 1)
            def _():
                if name[1] == 0:
                    far.wait_recv()
                attend_diag(0, name[1])

        else:
            attend_plane(*name[1:])

    def out_copy(hh, own):
        src = o_held.at[c if own else 1 - c, hh]
        dst = out_ref.at[0, :, columns(c + 2 * hh)]
        if own:
            return pltpu.make_async_copy(src, dst, local_sem.at[4 + hh])
        return remote(src, dst, count + 1 + hh, sibling)

    def out_wait(hh):
        dst = out_ref.at[0, :, columns(1 - c + 2 * hh)]
        return remote(o_held.at[c, hh], dst, count + 1 + hh, sibling)

    for hh in range(2):
        for pair in range(GROUP):
            for i in range(2):
                st, g = divmod(2 * pair + i, GROUP)
                both = acc[hh, pair, i * TOK : (i + 1) * TOK]
                o_held[st, hh, :, g * HD : (g + 1) * HD] = (
                    both[:, :HD] / both[:, HD:]
                ).astype(jnp.bfloat16)
        out_copy(hh, False).start()
        out_copy(hh, True).start()
    for name in plan:
        copy(name, False).wait_send()

    @pl.when(z_hi == 0)
    def _():
        far.wait_send()

    for hh in range(2):
        out_copy(hh, True).wait()
        out_copy(hh, False).wait_send()
        out_wait(hh).wait_recv()


def per_device(joined, drafted, queries, norm_gain, key_matrix, value_matrix):
    unit = {"A": 1, "B": 1, "C": 1}
    messages = 2 * len(gather_plan("w", unit, [])) + 4 + 3
    bf16 = jnp.bfloat16
    any_space = pl.BlockSpec(memory_space=pl.ANY)
    vmem = pl.BlockSpec(memory_space=pltpu.VMEM)
    dma = pltpu.SemaphoreType.DMA
    return pl.pallas_call(
        kernel,
        out_shape=jax.ShapeDtypeStruct((1, TOK, QH * HD), bf16),
        in_specs=[any_space, any_space, any_space, vmem, vmem, vmem],
        out_specs=any_space,
        scratch_shapes=[
            pltpu.VMEM((4, 4, 8, 80, HD), bf16),
            pltpu.VMEM((4, 4, 8, 64, HD), bf16),
            pltpu.VMEM((8, 4, 4, 80, HD), bf16),
            pltpu.VMEM((4, 4, 8, 2, KV_ROWS["A"], HD), bf16),
            pltpu.VMEM((4, 4, 8, 2, KV_ROWS["B"], HD), bf16),
            pltpu.VMEM((8, 4, 4, 2, KV_ROWS["C"], HD), bf16),
            pltpu.VMEM((STEPS, 2, 2, TOK, HD), bf16),
            pltpu.VMEM((2, TOK, D), bf16),
            pltpu.VMEM((3, TOK, D), bf16),
            pltpu.VMEM((2, 2, TOK, GROUP * HD), bf16),
            pltpu.VMEM((2, 2, TOK, GROUP * HD), bf16),
            pltpu.VMEM((2, GROUP, 2 * TOK, 2 * HD), jnp.float32),
            pltpu.VMEM((2, GROUP, 2 * TOK, HD), jnp.float32),
            pltpu.VMEM((2, 2 * TOK, 2 * HD), jnp.float32),
            pltpu.VMEM((TOK, 2 * HD), jnp.float32),
            pltpu.VMEM((1, D), jnp.float32),
            dma((6,)),
            dma((messages,)),
            dma((messages,)),
        ],
        compiler_params=pltpu.CompilerParams(
            collective_id=0, has_side_effects=True, vmem_limit_bytes=60 * 2**20
        ),
        cost_estimate=pl.CostEstimate(
            flops=17 * 10**9, bytes_accessed=8 * 10**6, transcendentals=3 * 10**7
        ),
        name="drafter",
    )(joined, drafted, queries, norm_gain, key_matrix, value_matrix)


def solution(mesh):
    placed = (
        P("seq", None),
        P("step", "seq", None),
        P("step", "seq", None),
        P(),
        P("seq", "step"),
        P("seq", "step"),
    )
    return jax.shard_map(
        per_device, mesh=mesh, in_specs=placed, out_specs=P("step", "seq", None), check_vma=False
    )
```

```python
import math

import jax
import jax.numpy as jnp
from jax import lax
from jax.experimental import pallas as pl
from jax.experimental.pallas import tpu as pltpu
from jax.sharding import PartitionSpec as P

QH = 28
KVH = 4
HD = 128
GROUP = QH // KVH
D = 7168
TOK = 128
STEPS = 4
ROWS = 112
SIZE = {"x": 4, "y": 4, "z": 8}
ORDER = {"A": "zyx", "B": "zxy", "C": "xyz"}
W_ROWS = {"A": 80, "B": 64, "C": 80}
KV_ROWS = {"A": 48, "B": 32, "C": 48}
KV_START = {"A": 0, "B": 48, "C": 80}
MESH = pl.DeviceIdType.MESH
LOG2E = math.log2(math.e)
NEG = -1e30


def position():
    step = lax.axis_index("step")
    seq = lax.axis_index("seq")
    return {
        "z": (step // 2) * 4 + seq // 16,
        "y": lax.rem(seq // 4, 4),
        "x": lax.rem(seq, 4),
        "core": lax.rem(step, 2),
    }


def device(at, **moved):
    at = dict(at)
    for axis, by in moved.items():
        size = SIZE.get(axis, 2)
        at[axis] = lax.rem(at[axis] + by + size, size)
    return (
        (at["z"] // 4) * 2 + at["core"],
        lax.rem(at["z"], 4) * 16 + at["y"] * 4 + at["x"],
    )


def hops(size):
    found = []
    for hop in range(1, size // 2):
        found += [(1, hop, None), (-1, hop, None)]
    last = size // 2
    return found + [(1, last, 0), (-1, last, 1)]


def near_first(size):
    return sorted(range(1, size), key=lambda k: min(k, size - k))


def gather_plan(tag, shard_bytes, begin):
    plan = {}
    for piece, (a1, a2, a3) in ORDER.items():
        n1, n2, n3 = SIZE[a1], SIZE[a2], SIZE[a3]
        unit = shard_bytes[piece]
        key = (tag, piece)
        first = [key + (1, 0, 1, k) for k in range(1, n1)]
        for k in near_first(n1):
            plan[key + (1, 0, 1, k)] = (
                (a1, 1 if k <= n1 // 2 else -1),
                unit * min(k, n1 - k),
                begin,
            )
        for d, k, half in hops(n2):
            need = [key + (2, 0, d, k - 1)] if k > 1 else first
            plan[key + (2, 0, d, k)] = ((a2, d), unit * n1 // (1 if half is None else 2), need)
        for sub in (0, 1, -1, 2):
            start = {
                0: first,
                1: [key + (2, 0, -1, 1)],
                -1: [key + (2, 0, 1, 1)],
                2: [key + (2, 0, 1, 2), key + (2, 0, -1, 2)],
            }[sub]
            if piece != "C" and sub == 0:
                start = start + [(tag, other, 1, 0, 1, k) for other in "AB" for k in range(1, n1)]
            elif piece != "C":
                other = "B" if piece == "A" else "A"
                start = start + [(tag, other, 2, 0, d, 1) for d in (1, -1)]
            for d, k, half in hops(n3):
                need = [key + (3, sub, d, k - 1)] if k > 1 else start
                plan[key + (3, sub, d, k)] = (
                    (a3, d),
                    unit * n1 // (1 if half is None else 2),
                    need,
                )
    return plan


def plane_needs(tag, piece, off):
    a1, a2, a3 = ORDER[piece]
    key = (tag, piece)
    if off == 0:
        return [key + (1, 0, 1, k) for k in range(1, SIZE[a1])] + [
            key + (2, 0, d, k) for d, k, _ in hops(SIZE[a2])
        ]
    return [
        key + (3, sub, d, k)
        for sub in (0, 1, -1, 2)
        for d, k, _ in hops(SIZE[a3])
        if (-d * k) % SIZE[a3] == off
    ]


LATENCY, RATE, CORE_RATE, HANDLE = 3.0, 42e3, 400e3, 0.05


def schedule(plan, tasks):
    steps = []
    done = set()
    link_free = {}
    arrive = {}
    unsent = dict(plan)
    todo = dict(tasks)
    now = 0.0

    def send_ready():
        for name in sorted(unsent, key=lambda name: (name[2], name[5])):
            link, size, need = plan[name]
            if all(other in done for other in need):
                del unsent[name]
                steps.append(("send", name))
                rate = CORE_RATE if link[0] == "core" else RATE
                begin = max(now, link_free.get(link, 0.0))
                link_free[link] = begin + size / rate
                arrive[name] = link_free[link] + LATENCY

    send_ready()
    while arrive or todo:
        early = min(arrive, key=lambda name: arrive[name], default=None)
        ready = next((t for t, (_, need) in todo.items() if all(o in done for o in need)), None)
        if early is not None and (arrive[early] <= now or ready is None):
            now = max(now, arrive.pop(early)) + HANDLE
            steps.append(("wait", early))
            done.add(early)
        else:
            now += todo.pop(ready)[0]
            steps.append(("task", ready))
            done.add(ready)
        send_ready()
    return steps, now


def kernel(
    joined_ref, drafted_ref, queries_ref, gain_ref, key_ref, value_ref, out_ref,
    wa, wb, wc, ka, kb, kc, diag, rows_in, normed, q_held, o_held, acc, top, proj, ctx,
    gain_held, local_sem, send_sem, recv_sem,
):
    at = position()
    x, y, z, c = at["x"], at["y"], at["z"], at["core"]
    step = lax.axis_index("step")
    seq = lax.axis_index("seq")
    z_hi = z // 4
    z_lo = lax.rem(z, 4)
    sibling = device(at, core=1)
    antipode = device(at, z=4)

    def columns(head):
        return pl.ds(pl.multiple_of(head * (GROUP * HD), HD), GROUP * HD)

    load_rows = [
        pltpu.make_async_copy(drafted_ref.at[0], rows_in.at[0], local_sem.at[0]),
        pltpu.make_async_copy(joined_ref, rows_in.at[1], local_sem.at[1]),
    ]
    load_q = [
        pltpu.make_async_copy(
            queries_ref.at[0, :, columns(c + 2 * hh)], q_held.at[c, hh], local_sem.at[2 + hh]
        )
        for hh in range(2)
    ]
    for load in load_rows + load_q:
        load.start()

    wa[x, y, z] = key_ref[0:80]
    wb[y, x, z, 0:32] = key_ref[80:ROWS]
    wb[y, x, z, 32:64] = value_ref[0:32]
    wc[z, y, x] = value_ref[32:ROWS]

    gain_held[...] = gain_ref[...].astype(jnp.float32).reshape(1, D)
    barrier = pltpu.get_barrier_semaphore()
    partners = [device(at, x=k) for k in range(1, 4)] + [device(at, z=k) for k in range(1, 8)]
    partners += [device(at, y=1), device(at, y=-1), sibling]
    for partner in partners:
        pl.semaphore_signal(barrier, inc=1, device_id=partner, device_id_type=MESH)
    pl.semaphore_wait(barrier, len(partners))

    plan = {}
    for i in range(2):
        plan["core", "q", 0, 0, 0, i] = (("core", 0), TOK * GROUP * HD * 2, [])
        plan["core", "rows", 0, 0, 0, i] = (("core", 0), TOK * D, [("norm", 0, i)])
    plan.update(
        gather_plan("w", {piece: rows * HD * 2 for piece, rows in W_ROWS.items()}, [])
    )
    plan.update(
        gather_plan(
            "kv", {piece: 2 * rows * HD * 2 for piece, rows in KV_ROWS.items()}, [("project", 0)]
        )
    )
    index = {name: i for i, name in enumerate(plan)}
    bufs = {
        ("w", "A"): wa, ("w", "B"): wb, ("w", "C"): wc,
        ("kv", "A"): ka, ("kv", "B"): kb, ("kv", "C"): kc,
    }

    def remote(src, dst, i, target):
        return pltpu.make_async_remote_copy(
            src_ref=src,
            dst_ref=dst,
            send_sem=send_sem.at[i],
            recv_sem=recv_sem.at[i],
            device_id=target,
            device_id_type=MESH,
        )

    def copy(name, incoming):
        tag, piece, phase, sub, d, k = name
        i = index[name]
        if tag == "core":
            mine = 1 - c if incoming else c
            if piece == "rows":
                ref = normed.at[mine, pl.ds(k * 64, 64)]
                return remote(ref, ref, i, sibling)
            src = queries_ref.at[0, :, columns(1 - c + 2 * k)]
            return remote(src, q_held.at[mine, k], i, sibling)
        buf = bufs[tag, piece]
        a1, a2, a3 = ORDER[piece]
        axis = ORDER[piece][phase - 1]
        n, n1 = SIZE[axis], SIZE[a1]
        q = lax.rem(at[axis] - d * (k if incoming else k - 1) + n, n)
        half = None
        if phase > 1 and k == n // 2:
            half = 0 if d > 0 else 1
        inner = pl.ds(0, n1) if half is None else pl.ds(half * (n1 // 2), n1 // 2)
        if phase == 1:
            mine = lax.rem(at[axis] - k + n, n) if incoming else at[axis]
            ref = buf.at[at[a3], at[a2], mine]
            return remote(ref, ref, i, device(at, **{axis: k}))
        if phase == 2:
            ref = buf.at[at[a3], q, inner]
        else:
            ref = buf.at[q, lax.rem(at[a2] + sub + SIZE[a2], SIZE[a2]), inner]
        return remote(ref, ref, i, device(at, **{axis: d}))

    count = len(plan)
    far = remote(diag.at[pl.ds(0, 2)], diag.at[pl.ds(0, 2)], count, antipode)

    def norm(which, first):
        if first == 0:
            load_rows[which].wait()

        def body(i, carry):
            start = pl.multiple_of(first + i * 16, 16)
            rows = rows_in[which, pl.ds(start, 16), :].astype(jnp.float32)
            mean = jnp.sum(rows * rows, axis=-1, keepdims=True) * (1.0 / D)
            scaled = rows * lax.rsqrt(mean + 1e-06)
            done = (scaled * gain_held[...]).astype(jnp.bfloat16)
            normed[c if which == 0 else 2, pl.ds(start, 16), :] = done
            return carry

        lax.fori_loop(0, 4, body, 0)

    def project():
        proj[...] = jnp.zeros_like(proj)
        ctx[...] = jnp.zeros_like(ctx)

        def part(zz, carry):
            hh = zz // 4
            cols = pl.ds(pl.multiple_of(lax.rem(zz, 4) * (16 * ROWS), 128), 16 * ROWS)
            keys, values = [], []
            for yy in range(4):
                for xx in range(4):
                    keys += [wa[xx, yy, zz], wb[yy, xx, zz, 0:32]]
                    values += [wb[yy, xx, zz, 32:64], wc[zz, yy, xx]]
            both = jnp.concatenate(
                [jnp.concatenate(keys, axis=0), jnp.concatenate(values, axis=0)], axis=1
            )
            drafted_part = normed[0:2, :, cols].reshape(2 * TOK, 16 * ROWS)
            proj[hh] += jnp.dot(drafted_part, both, preferred_element_type=jnp.float32)

            @pl.when(hh == z_hi)
            def _():
                ctx[...] += jnp.dot(normed[2, :, cols], both, preferred_element_type=jnp.float32)

            return carry

        lax.fori_loop(0, 8, part, 0)
        held = ctx[...].astype(jnp.bfloat16)
        for kv in range(2):
            part = held[:, kv * HD : (kv + 1) * HD]
            ka[x, y, z, kv] = part[0:48]
            kb[y, x, z, kv] = part[48:80]
            kc[z, y, x, kv] = part[80:128]
        for st in range(2):
            for hh in range(2):
                both = proj[hh, pl.ds(st * TOK, TOK)].astype(jnp.bfloat16)
                for kv in range(2):
                    diag[2 * z_hi + st, hh, kv] = both[:, kv * HD : (kv + 1) * HD]

    def send_far():
        @pl.when(z_hi == 0)
        def _():
            far.start()

    scale = LOG2E * HD ** (-0.5)
    row = lax.broadcasted_iota(jnp.int32, (TOK, 1), 0)

    def attend(hh, keys, values, bias):
        count = keys.shape[0]
        wide = jnp.concatenate([values, jnp.ones((count, HD), jnp.bfloat16)], axis=1)

        def score(pair):
            tiles = [divmod(2 * pair + i, GROUP) for i in range(2)]
            q = jnp.concatenate(
                [q_held[st, hh, :, g * HD : (g + 1) * HD] for st, g in tiles], axis=0
            )
            scores = lax.dot_general(
                q, keys, (((1,), (1,)), ((), ())), preferred_element_type=jnp.float32
            ) * scale + jnp.concatenate([bias[st] for st, _ in tiles], axis=0)
            old = top[hh, pair]
            new = jnp.maximum(old, jnp.max(scores, axis=-1, keepdims=True))
            top[hh, pair] = new
            return scores, old, new

        def weigh(pair, scores, old, new):
            fade = jnp.exp2(old - new)
            p = jnp.exp2(scores - jnp.concatenate([new] * (count // HD), axis=1))
            acc[hh, pair] = acc[hh, pair] * jnp.concatenate([fade, fade], axis=1) + jnp.dot(
                p.astype(jnp.bfloat16), wide, preferred_element_type=jnp.float32
            )

        held = score(0)
        for pair in range(GROUP):
            following = score(pair + 1) if pair + 1 < GROUP else None
            weigh(pair, *held)
            held = following

    def attend_diag(pair, hh):
        keys, values = (
            diag[pl.ds(2 * pair, 2), hh, kv].reshape(2 * TOK, HD) for kv in range(2)
        )
        col = lax.broadcasted_iota(jnp.int32, (TOK, 2 * TOK), 1)
        j = 2 * pair + col // TOK

        own = lax.rem(col, TOK) == row
        bias = [
            jnp.where(jnp.logical_and(own, j <= 2 * z_hi + st), 0.0, NEG) for st in range(2)
        ]
        attend(hh, keys, values, bias)

    def attend_plane(piece, off):
        rows = KV_ROWS[piece]
        count = 16 * rows
        col = lax.broadcasted_iota(jnp.int32, (1, count), 1)
        shard = col // rows
        outer, inner = shard // 4, lax.rem(shard, 4)
        if piece == "C":
            zed = lax.rem(z + off, 8)
            hh = zed // 4
            keys, values = (kc[zed, :, :, kv].reshape(count, HD) for kv in range(2))
            where = (lax.rem(zed, 4), outer, inner)
        else:
            plane = lax.rem(at[ORDER[piece][2]] + off, 4)
            buf = ka if piece == "A" else kb
            where = (inner, outer, plane) if piece == "A" else (inner, plane, outer)
        zz, yy, xx = where
        key_at = (zz * 16 + yy * 4 + xx) * TOK + KV_START[piece] + lax.rem(col, rows)
        bias = [jnp.where(key_at <= seq * TOK + row, 0.0, NEG)] * 2
        if piece == "C":

            @pl.when(zz <= z_lo)
            def _():
                attend(hh, keys, values, bias)

        else:

            def head(hh, carry):
                keys, values = (
                    buf[plane, :, pl.ds(4 * hh, 4), kv].reshape(count, HD) for kv in range(2)
                )
                attend(hh, keys, values, bias)
                return carry

            lax.fori_loop(0, 2, head, 0)

    tasks = {}
    for which in range(2):
        for i in range(2):
            tasks["norm", which, i] = (2.2, [])
    tasks["project", 0] = (
        5.0,
        list(tasks)
        + [name for name in plan if name[0] == "w"]
        + [name for name in plan if name[:2] == ("core", "rows")],
    )
    tasks["far", 0] = (0.1, [("project", 0), ("kv", "A", 2, 0, 1, 2)])
    for hh in range(2):
        tasks["diag", hh] = (0.8, [("project", 0)])
    for off in (0, 1, -1, 2, -2, 3, -3, 4):
        for piece in "ABC":
            if piece == "C" or -2 < off < 3:
                need = plane_needs("kv", piece, off % SIZE[ORDER[piece][2]])
                cost = KV_ROWS[piece] / 48 * (1.75 if piece == "C" else 3.5)
                tasks["attend", piece, off % SIZE[ORDER[piece][2]]] = (cost, need)
    for hh in range(2):
        tasks["diag far", hh] = (0.8, [("far", 0), ("kv", "C", 3, 2, 1, 3)])

    steps, _ = schedule(plan, tasks)
    acc[...] = jnp.zeros_like(acc)
    top[...] = jnp.full_like(top, NEG)
    for kind, name in steps:
        if kind == "send":
            copy(name, False).start()
        elif kind == "wait":
            copy(name, True).wait_recv()
        elif name[0] == "norm":
            norm(name[1], 64 * name[2])
        elif name[0] == "project":
            project()
        elif name[0] == "far":
            send_far()
        elif name[0] == "diag":
            if name[1] == 0:
                for load in load_q:
                    load.wait()
            attend_diag(z_hi, name[1])
        elif name[0] == "diag far":

            @pl.when(z_hi == 1)
            def _():
                if name[1] == 0:
                    far.wait_recv()
                attend_diag(0, name[1])

        else:
            attend_plane(*name[1:])

    def out_copy(hh, own):
        src = o_held.at[c if own else 1 - c, hh]
        dst = out_ref.at[0, :, columns(c + 2 * hh)]
        if own:
            return pltpu.make_async_copy(src, dst, local_sem.at[4 + hh])
        return remote(src, dst, count + 1 + hh, sibling)

    def out_wait(hh):
        dst = out_ref.at[0, :, columns(1 - c + 2 * hh)]
        return remote(o_held.at[c, hh], dst, count + 1 + hh, sibling)

    for hh in range(2):
        for pair in range(GROUP):
            for i in range(2):
                st, g = divmod(2 * pair + i, GROUP)
                both = acc[hh, pair, i * TOK : (i + 1) * TOK]
                o_held[st, hh, :, g * HD : (g + 1) * HD] = (
                    both[:, :HD] / both[:, HD:]
                ).astype(jnp.bfloat16)
        out_copy(hh, False).start()
        out_copy(hh, True).start()
    for name in plan:
        copy(name, False).wait_send()

    @pl.when(z_hi == 0)
    def _():
        far.wait_send()

    for hh in range(2):
        out_copy(hh, True).wait()
        out_copy(hh, False).wait_send()
        out_wait(hh).wait_recv()


def per_device(joined, drafted, queries, norm_gain, key_matrix, value_matrix):
    unit = {"A": 1, "B": 1, "C": 1}
    messages = 2 * len(gather_plan("w", unit, [])) + 4 + 3
    bf16 = jnp.bfloat16
    any_space = pl.BlockSpec(memory_space=pl.ANY)
    vmem = pl.BlockSpec(memory_space=pltpu.VMEM)
    dma = pltpu.SemaphoreType.DMA
    return pl.pallas_call(
        kernel,
        out_shape=jax.ShapeDtypeStruct((1, TOK, QH * HD), bf16),
        in_specs=[any_space, any_space, any_space, vmem, vmem, vmem],
        out_specs=any_space,
        scratch_shapes=[
            pltpu.VMEM((4, 4, 8, 80, HD), bf16),
            pltpu.VMEM((4, 4, 8, 64, HD), bf16),
            pltpu.VMEM((8, 4, 4, 80, HD), bf16),
            pltpu.VMEM((4, 4, 8, 2, KV_ROWS["A"], HD), bf16),
            pltpu.VMEM((4, 4, 8, 2, KV_ROWS["B"], HD), bf16),
            pltpu.VMEM((8, 4, 4, 2, KV_ROWS["C"], HD), bf16),
            pltpu.VMEM((STEPS, 2, 2, TOK, HD), bf16),
            pltpu.VMEM((2, TOK, D), bf16),
            pltpu.VMEM((3, TOK, D), bf16),
            pltpu.VMEM((2, 2, TOK, GROUP * HD), bf16),
            pltpu.VMEM((2, 2, TOK, GROUP * HD), bf16),
            pltpu.VMEM((2, GROUP, 2 * TOK, 2 * HD), jnp.float32),
            pltpu.VMEM((2, GROUP, 2 * TOK, HD), jnp.float32),
            pltpu.VMEM((2, 2 * TOK, 2 * HD), jnp.float32),
            pltpu.VMEM((TOK, 2 * HD), jnp.float32),
            pltpu.VMEM((1, D), jnp.float32),
            dma((6,)),
            dma((messages,)),
            dma((messages,)),
        ],
        compiler_params=pltpu.CompilerParams(
            collective_id=0, has_side_effects=True, vmem_limit_bytes=60 * 2**20
        ),
        cost_estimate=pl.CostEstimate(
            flops=17 * 10**9, bytes_accessed=8 * 10**6, transcendentals=3 * 10**7
        ),
        name="drafter",
    )(joined, drafted, queries, norm_gain, key_matrix, value_matrix)


def solution(mesh):
    placed = (
        P("seq", None),
        P("step", "seq", None),
        P("step", "seq", None),
        P(),
        P("seq", "step"),
        P("seq", "step"),
    )
    return jax.shard_map(
        per_device, mesh=mesh, in_specs=placed, out_specs=P("step", "seq", None), check_vma=False
    )
```
